128 devices in a mesh: row: 8 (over z_hi, x), col: 16 (over z_lo, y, core).
Axes of the slice: x: 4, y: 4, z: 4 (z_hi: 2, z_lo: 2; z = z_hi * 2 + z_lo), core: 2. Of those that a mesh axis runs over, the one named last changes fastest.
Arguments:
- subspace: bfloat16 [65536, 128], P(('row', 'col')), may hold values from -6 to 6
- blocks: bfloat16 [8, 16, 512, 128, 128], P('row', 'col'), may hold values from -0.0625 to 0.0625
- row_pointer: int32 [8, 16, 65], P('row', 'col'), may hold values from 0 to 512, as said below
- block_column: int32 [8, 16, 512], P('row', 'col'), may hold values from 0 to 31, as said below
Outputs:
- filtered: float32 [65536, 128], P(('row', 'col'))
The draws below stay inside these ranges and needn't reach their ends.
Inputs may be any that keep to these rules, and one draw needn't show every extreme that they name: `row_pointer`: each tile's pointers start at 0 and rise by 1 to 12 a block row; a tile's last pointer, its count of live blocks, is 128 or 512, and some tile holds 512 in every draw. `block_column`: local block columns are distinct within a block row; slots beyond a tile's count hold 0.
All inputs are finite; a program needn't handle non-finite values.
Results may differ from the reference program's by a relative error of at most 0.003.
Values may be sent and summed in bfloat16 or wider, within the bound.
No kernel may reach another device: no remote copies, remote signals or barrier semaphores. Data moves between devices by JAX's collectives and lax.ppermute only.
A program may use at most 128 MiB of HBM per device.

```python
import jax
import jax.numpy as jnp
from jax import lax

BS = 128
K = 128
PB = 4
HEAVY = 8
ROWGRID = 8
COLGRID = 16
TROWS = 64
TCOLS = 32
CAP = 512
NROWS = 65536


def pattern(key):
    tiles = ROWGRID * COLGRID
    keys = jax.random.split(key, 4)
    heavy = jax.random.randint(keys[0], (tiles,), 0, 8) == 0
    forced = jax.random.randint(keys[1], (), 0, tiles)
    heavy = heavy | (jnp.arange(tiles, dtype=jnp.int32) == forced)
    per_row = jnp.where(heavy, HEAVY, HEAVY // 4).astype(jnp.int32)
    spread = per_row // 2
    raw_draw = jax.random.randint(keys[2], (tiles, TROWS // 2), 0, 1 << 20)
    deltas = raw_draw % (2 * spread + 1)[:, None] - spread[:, None]
    counts = jnp.stack([per_row[:, None] + deltas, per_row[:, None] - deltas], axis=-1).reshape(tiles, TROWS)
    pointer = jnp.concatenate([jnp.zeros((tiles, 1), jnp.int32), jnp.cumsum(counts, axis=1).astype(jnp.int32)], axis=1)
    scores = jax.random.randint(keys[3], (tiles, TROWS, TCOLS), 0, 1 << 20) * TCOLS + jnp.arange(TCOLS, dtype=jnp.int32)
    orders = jnp.argsort(scores, axis=-1).astype(jnp.int32).reshape(tiles, TROWS * TCOLS)
    positions = jnp.arange(CAP, dtype=jnp.int32)
    row_ids = jnp.sum((pointer[:, None, 1:] <= positions[None, :, None]).astype(jnp.int32), axis=2)
    row_ids = jnp.minimum(row_ids, TROWS - 1)
    row_starts = jnp.take_along_axis(pointer, row_ids, axis=1)
    offsets = jnp.clip(positions[None, :] - row_starts, 0, TCOLS - 1)
    columns = jnp.take_along_axis(orders, row_ids * TCOLS + offsets, axis=1)
    columns = jnp.where(positions[None, :] < pointer[:, TROWS:], columns, 0).astype(jnp.int32)
    return (pointer.reshape(ROWGRID, COLGRID, TROWS + 1), columns.reshape(ROWGRID, COLGRID, CAP))


def draw_row_pointer(key, part):
    shared = pattern(jax.random.fold_in(key, 11))
    return shared[0]


def draw_block_column(key, part):
    shared = pattern(jax.random.fold_in(key, 11))
    return shared[1]


def level_of(rng, shape, shards, least, high):
    level = 1.0
    for axis_at, blocks in shards:
        heights = jax.random.uniform(jax.random.fold_in(jax.random.fold_in(rng, 6), axis_at), (blocks,), jnp.float32, least / len(shards), high / len(shards))
        level = level * jnp.repeat(jnp.exp(heights), shape[axis_at] // blocks).reshape((-1,) + (1,) * (len(shape) - 1 - axis_at))
    return level


def gaussian(stream_key, dims, width, bound, cuts=(), held_as=jnp.bfloat16):
    entries = jax.random.normal(stream_key, dims, jnp.float32) * width
    if len(cuts) > 0:
        entries = level_of(stream_key, dims, cuts, -0.22, 0.18) * entries
    return jnp.clip(entries, min=-bound, max=bound).astype(held_as)


def setup_inputs(seed: int = 0) -> dict:
    splits = jax.random.split(jax.random.key(seed), 5)
    subspace = gaussian(splits[0], (NROWS, K), 1.0, 6.0, ((0, 128),))
    blocks = gaussian(splits[1], (ROWGRID, COLGRID, CAP, BS, BS), (COLGRID * HEAVY * BS // 2) ** -0.5, 0.0625, ((0, 8), (1, 16)))
    row_pointer = draw_row_pointer(jax.random.fold_in(splits[4], 71), 0)
    block_column = draw_block_column(jax.random.fold_in(splits[4], 71), 0)
    return {"subspace": subspace, "blocks": blocks, "row_pointer": row_pointer, "block_column": block_column}


def tile_product(tile_blocks, pointer, columns, gathered):
    positions = jnp.arange(CAP, dtype=jnp.int32)
    row_ids = jnp.sum((pointer[1:][None, :] <= positions[:, None]).astype(jnp.int32), axis=1)
    row_ids = jnp.minimum(row_ids, TROWS - 1)
    is_live = positions < pointer[TROWS]
    picked = gathered[columns]
    product = jnp.einsum("jab,jbk->jak", tile_blocks.astype(jnp.float32), picked.astype(jnp.float32))
    product = jnp.where(is_live[:, None, None], product, 0.0)
    summed = jax.ops.segment_sum(product, row_ids, num_segments=TROWS)
    return summed.reshape(TROWS * BS, K)


def multiply(vector, blocks, row_pointer, block_column):
    pieces = vector.reshape(ROWGRID, COLGRID, PB * BS, K)
    by_column = jnp.transpose(pieces, (1, 0, 2, 3)).reshape(COLGRID, TCOLS, BS, K)
    column_ids = jnp.tile(jnp.arange(COLGRID, dtype=jnp.int32), ROWGRID)

    def one_tile(item):
        tile_blocks, pointer, columns, column_id = item
        gathered = by_column[column_id]
        return tile_product(tile_blocks, pointer, columns, gathered).astype(jnp.float32)

    terms = lax.map(one_tile, (blocks.reshape(ROWGRID * COLGRID, CAP, BS, BS),
                               row_pointer.reshape(ROWGRID * COLGRID, TROWS + 1),
                               block_column.reshape(ROWGRID * COLGRID, CAP), column_ids))
    terms = terms.reshape(ROWGRID, COLGRID, TROWS * BS, K)
    return jnp.sum(terms, axis=1).reshape(NROWS, K)


def reference(subspace, blocks, row_pointer, block_column):
    first = multiply(subspace, blocks, row_pointer, block_column).astype(jnp.bfloat16)
    second = (2.0 * multiply(first, blocks, row_pointer, block_column) - subspace.astype(jnp.float32)).astype(jnp.bfloat16)
    return 2.0 * multiply(second, blocks, row_pointer, block_column) - first.astype(jnp.float32)
```

```python
import functools

import jax
import jax.numpy as jnp
from jax import lax
from jax.experimental import pallas as pl
from jax.experimental.pallas import tpu as pltpu
from jax.sharding import PartitionSpec as P

UNROLL = 8
MIB = 1024 * 1024


def pair_list(core_ref, pointer_ref, column_ref, word_ref, count_ref, *, groups, height, capacity):
    core = core_ref[0]
    for half in range(2):
        which = core if half else 1 - core

        def one_row(local, number):
            row = (2 * (local // height) + which) * height + local % height
            first, last = pointer_ref[row], pointer_ref[row + 1]

            def one_pair(k, _):
                j = first + 2 * k
                next_j = jnp.minimum(j + 1, capacity - 1)
                both = (j + 1 < last).astype(jnp.int32)
                word_ref[half, number + k] = (
                    j + local * 512 + column_ref[j] * 16384 + column_ref[next_j] * 524288 + (1 + both) * 16777216
                )
                return 0

            pairs = (last - first + 1) // 2
            lax.fori_loop(0, pairs, one_pair, 0)
            return number + pairs

        total = lax.fori_loop(0, groups * height, one_row, 0)
        for k in range(UNROLL):
            word_ref[half, total + k] = 0
        count_ref[half] = (total + UNROLL - 1) // UNROLL


def make_lists(core, pointer, columns, height):
    capacity = columns.shape[0]
    rows = pointer.shape[0] - 1
    groups = rows // height // 2
    smem = pl.BlockSpec(memory_space=pltpu.SMEM)
    width = (rows // 2) * 6 + UNROLL
    return pl.pallas_call(
        functools.partial(pair_list, groups=groups, height=height, capacity=capacity),
        in_specs=[smem] * 3,
        out_specs=[smem] * 2,
        out_shape=[jax.ShapeDtypeStruct((2, width), jnp.int32), jax.ShapeDtypeStruct((2,), jnp.int32)],
        name="pair_list",
    )(core, pointer, columns)


def half_kernel(word_ref, count_ref, vector_ref, block_ref, out_ref, *, half):
    out_ref[...] = jnp.zeros_like(out_ref)
    capacity = block_ref.shape[0]

    def body(step, _):
        for k in range(UNROLL):
            word = word_ref[half, step * UNROLL + k]
            j = word & 511
            row = (word >> 9) & 31
            c1 = (word >> 14) & 31
            c2 = (word >> 19) & 31
            n = word >> 24
            left = jnp.concatenate([block_ref[j], block_ref[jnp.minimum(j + 1, capacity - 1)]], axis=1)
            v1 = vector_ref[c1]
            v2 = vector_ref[c2]
            right = jnp.concatenate([jnp.where(n > 0, v1, jnp.zeros_like(v1)), jnp.where(n > 1, v2, jnp.zeros_like(v2))], axis=0)
            out_ref[row] += jnp.dot(left, right, preferred_element_type=jnp.float32)
        return 0

    lax.fori_loop(0, count_ref[half], body, 0)


def half_terms(words, counts, vector, tile_blocks, half):
    smem = pl.BlockSpec(memory_space=pltpu.SMEM)
    vmem = pl.BlockSpec(memory_space=pltpu.VMEM)
    size = tile_blocks.shape[1]
    return pl.pallas_call(
        functools.partial(half_kernel, half=half),
        in_specs=[smem, smem, vmem, vmem],
        out_specs=vmem,
        out_shape=jax.ShapeDtypeStruct((32, size, vector.shape[2]), jnp.float32),
        compiler_params=pltpu.CompilerParams(vmem_limit_bytes=24 * MIB),
        name="half_terms",
    )(words, counts, vector, tile_blocks)


def per_device(subspace, blocks, row_pointer, block_column):
    tile_blocks = blocks[0, 0]
    size = tile_blocks.shape[1]
    own_rows, width = subspace.shape
    height = own_rows // size
    chips = lax.axis_size("col") // 2
    core = lax.axis_index("col") % 2
    swap = [(c, c ^ 1) for c in range(2 * chips)]
    alike = [[2 * d + k for d in range(chips)] for k in range(2)]
    sources = lax.axis_size("row")
    words, counts = make_lists(core.reshape(1), row_pointer[0, 0], block_column[0, 0], height)

    def multiply(vector):
        spread = jnp.broadcast_to(vector[None], (sources, own_rows, width))
        gathered = lax.all_to_all(spread, "row", 0, 0).reshape(-1, size, width)
        given = half_terms(words, counts, gathered, tile_blocks, 0)
        taken = lax.ppermute(given, "col", swap)
        kept = half_terms(words, counts, gathered, tile_blocks, 1)
        both = (kept + taken).reshape(chips, own_rows, width)
        most = jnp.max(jnp.abs(both), axis=(1, 2), keepdims=True)
        power = jnp.floor(jnp.log2(jnp.maximum(most, 1e-30))) - 14.0
        scaled = (both * jnp.exp2(-power)).astype(jnp.float16)
        tag = jnp.broadcast_to(power.astype(jnp.float16), (chips, 8, width))
        parts = lax.all_to_all(
            jnp.concatenate([scaled, tag], axis=1), "col", 0, 0, axis_index_groups=alike
        )
        weight = jnp.exp2(parts[:, own_rows : own_rows + 1, :1].astype(jnp.float32))
        return jnp.sum(parts[:, :own_rows].astype(jnp.float32) * weight, axis=0)

    first = multiply(subspace).astype(jnp.bfloat16)
    second = (2.0 * multiply(first) - subspace.astype(jnp.float32)).astype(jnp.bfloat16)
    return 2.0 * multiply(second) - first.astype(jnp.float32)


def solution(mesh):
    placed = (
        P(("row", "col"), None),
        P("row", "col", None, None, None),
        P("row", "col", None),
        P("row", "col", None),
    )
    return jax.shard_map(
        per_device, mesh=mesh, in_specs=placed, out_specs=P(("row", "col"), None), check_vma=False
    )
```

```python
import functools

import jax
import jax.numpy as jnp
from jax import lax
from jax.experimental import pallas as pl
from jax.experimental.pallas import tpu as pltpu
from jax.sharding import PartitionSpec as P

UNROLL = 24
PARTS = 16
MOST = 12
MIB = 1024 * 1024


def pair_list(core_ref, pointer_ref, column_ref, word_ref, count_ref, *, groups, height):
    core = core_ref[0]
    for half in range(2):
        which = core if half else 1 - core

        def one_row(local, number):
            row = (2 * (local // height) + which) * height + local % height
            first, last = pointer_ref[row], pointer_ref[row + 1]

            def one_pair(k, _):
                j = first + 2 * k
                both = (j + 1 < last).astype(jnp.int32)
                word_ref[half, number + k] = (
                    j + local * 512 + column_ref[j] * 16384 + column_ref[j + both] * 524288 + (1 + both) * 16777216
                )
                return 0

            pairs = (last - first + 1) // 2
            lax.fori_loop(0, pairs, one_pair, 0)
            return number + pairs

        total = lax.fori_loop(0, groups * height, one_row, 0)
        for k in range(UNROLL):
            word_ref[half, total + k] = word_ref[half, total - 1] & 16383
        count_ref[half] = (total + UNROLL - 1) // UNROLL


def make_lists(core, pointer, columns, height):
    rows = pointer.shape[0] - 1
    groups = rows // height // 2
    smem = pl.BlockSpec(memory_space=pltpu.SMEM)
    width = (rows // 2) * (MOST // 2) + UNROLL
    return pl.pallas_call(
        functools.partial(pair_list, groups=groups, height=height),
        in_specs=[smem] * 3,
        out_specs=[smem] * 2,
        out_shape=[jax.ShapeDtypeStruct((2, width), jnp.int32), jax.ShapeDtypeStruct((2,), jnp.int32)],
        compiler_params=pltpu.CompilerParams(vmem_limit_bytes=2 * MIB),
        name="pair_list",
    )(core, pointer, columns)


def add_pairs(word_ref, count_ref, vector_ref, block_ref, out_ref, half, ready, arrive):
    out_ref[...] = jnp.zeros_like(out_ref)

    def body(step, ready):
        ready = arrive((word_ref[half, step * UNROLL + UNROLL - 1] & 511) + 1, ready)
        for k in range(UNROLL):
            word = word_ref[half, step * UNROLL + k]
            j = word & 511
            row = (word >> 9) & 31
            c1 = (word >> 14) & 31
            c2 = (word >> 19) & 31
            n = word >> 24
            left = jnp.concatenate([block_ref[j], block_ref[j + (n >> 1)]], axis=1)
            v1 = vector_ref[c1]
            v2 = vector_ref[c2]
            right = jnp.concatenate([jnp.where(n > 0, v1, jnp.zeros_like(v1)), jnp.where(n > 1, v2, jnp.zeros_like(v2))], axis=0)
            out_ref[row] += jnp.dot(left, right, preferred_element_type=jnp.float32)
        return ready

    return lax.fori_loop(0, count_ref[half], body, ready)


def given_kernel(pointer_ref, word_ref, count_ref, vector_ref, source_ref, out_ref, block_ref, sem):
    step = source_ref.shape[0] // PARTS
    used = (pointer_ref[pointer_ref.shape[0] - 1] + step - 1) // step

    def copy(k):
        part = pl.ds(k * step, step)
        return pltpu.make_async_copy(source_ref.at[part], block_ref.at[part], sem.at[k])

    def start(k, _):
        copy(k).start()
        return 0

    def wait(k, _):
        copy(k).wait()
        return 0

    def arrive(last, ready):
        needed = jnp.maximum(jnp.minimum(last // step + 1, used), ready)
        lax.fori_loop(ready, needed, wait, 0)
        return needed

    lax.fori_loop(0, used, start, 0)
    ready = add_pairs(word_ref, count_ref, vector_ref, block_ref, out_ref, 0, 0, arrive)
    lax.fori_loop(ready, used, wait, 0)


def half_kernel(word_ref, count_ref, vector_ref, block_ref, out_ref, *, half):
    add_pairs(word_ref, count_ref, vector_ref, block_ref, out_ref, half, 0, lambda last, ready: ready)


def given_terms(pointer, words, counts, vector, tile_blocks):
    smem = pl.BlockSpec(memory_space=pltpu.SMEM)
    vmem = pl.BlockSpec(memory_space=pltpu.VMEM)
    return pl.pallas_call(
        given_kernel,
        in_specs=[smem, smem, smem, vmem, pl.BlockSpec(memory_space=pl.ANY)],
        out_specs=[vmem, vmem],
        out_shape=[
            jax.ShapeDtypeStruct((vector.shape[0], tile_blocks.shape[1], vector.shape[2]), jnp.float32),
            pltpu.VMEM(tile_blocks.shape, tile_blocks.dtype),
        ],
        scratch_shapes=[pltpu.SemaphoreType.DMA((PARTS,))],
        compiler_params=pltpu.CompilerParams(vmem_limit_bytes=24 * MIB),
        name="given_terms",
    )(pointer, words, counts, vector, pltpu.with_memory_space_constraint(tile_blocks, pltpu.HBM))


def half_terms(words, counts, vector, held, half):
    smem = pl.BlockSpec(memory_space=pltpu.SMEM)
    vmem = pl.BlockSpec(memory_space=pltpu.VMEM)
    return pl.pallas_call(
        functools.partial(half_kernel, half=half),
        in_specs=[smem, smem, vmem, vmem],
        out_specs=vmem,
        out_shape=jax.ShapeDtypeStruct((vector.shape[0], held.shape[1], vector.shape[2]), jnp.float32),
        compiler_params=pltpu.CompilerParams(vmem_limit_bytes=24 * MIB),
        name="half_terms",
    )(words, counts, vector, pltpu.with_memory_space_constraint(held, pltpu.VMEM))


def combine_kernel(kept_ref, taken_ref, out_ref):
    chips, taller, width = out_ref.shape
    rows, size, _ = kept_ref.shape
    height = rows // chips
    step = 32
    tops = []
    for chip in range(chips):
        most = jnp.zeros((step, width), jnp.float32)
        for k in range(height):
            row = chip * height + k
            for t in range(0, size, step):
                both = kept_ref[row, t : t + step] + taken_ref[row, t : t + step]
                out_ref[chip, k * size + t : k * size + t + step] = both
                most = jnp.maximum(most, jnp.abs(both))
        tops.append(jnp.max(most, axis=0, keepdims=True))
    most = jnp.max(jnp.concatenate(tops, axis=0), axis=1, keepdims=True)
    power = jnp.floor(jnp.log2(jnp.maximum(most, 1e-30))) - 14.0
    power = jnp.broadcast_to(power, (chips, width))
    scale = jnp.exp2(-power)
    for chip in range(chips):
        by = jnp.broadcast_to(scale[chip : chip + 1], (step, width))
        for t in range(0, height * size, step):
            out_ref[chip, t : t + step] = out_ref[chip, t : t + step] * by
        out_ref[chip, height * size :] = jnp.broadcast_to(power[chip : chip + 1], (taller - height * size, width))


def combine(kept, taken, chips):
    vmem = pl.BlockSpec(memory_space=pltpu.VMEM)
    rows, size, width = kept.shape
    return pl.pallas_call(
        combine_kernel,
        in_specs=[vmem, vmem],
        out_specs=vmem,
        out_shape=jax.ShapeDtypeStruct((chips, rows // chips * size + 8, width), jnp.float32),
        compiler_params=pltpu.CompilerParams(vmem_limit_bytes=24 * MIB),
        name="combine",
    )(kept, taken)


def per_device(subspace, blocks, row_pointer, block_column):
    tile_blocks = blocks[0, 0]
    pointer = row_pointer[0, 0]
    size = tile_blocks.shape[1]
    own_rows, width = subspace.shape
    height = own_rows // size
    chips = lax.axis_size("col") // 2
    core = lax.axis_index("col") % 2
    swap = [(c, c ^ 1) for c in range(2 * chips)]
    alike = [[2 * d + k for d in range(chips)] for k in range(2)]
    sources = lax.axis_size("row")
    words, counts = make_lists(core.reshape(1), pointer, block_column[0, 0], height)

    def multiply(vector, held):
        spread = jnp.broadcast_to(vector[None], (sources, own_rows, width))
        gathered = lax.all_to_all(spread, "row", 0, 0).reshape(-1, size, width)
        if held is None:
            given, held = given_terms(pointer, words, counts, gathered, tile_blocks)
        else:
            given = half_terms(words, counts, gathered, held, 0)
        taken = lax.ppermute(given, "col", swap)
        kept = half_terms(words, counts, gathered, held, 1)
        scaled = combine(kept, taken, chips).astype(jnp.float16)
        parts = lax.all_to_all(scaled, "col", 0, 0, axis_index_groups=alike)
        weight = jnp.exp2(parts[:, own_rows : own_rows + 1, :1].astype(jnp.float32))
        return jnp.sum(parts[:, :own_rows].astype(jnp.float32) * weight, axis=0), held

    total, held = multiply(subspace, None)
    first = total.astype(jnp.bfloat16)
    total, held = multiply(first, held)
    second = (2.0 * total - subspace.astype(jnp.float32)).astype(jnp.bfloat16)
    total, held = multiply(second, held)
    return 2.0 * total - first.astype(jnp.float32)


def solution(mesh):
    placed = (
        P(("row", "col"), None),
        P("row", "col", None, None, None),
        P("row", "col", None),
        P("row", "col", None),
    )
    return jax.shard_map(
        per_device, mesh=mesh, in_specs=placed, out_specs=P(("row", "col"), None), check_vma=False
    )
```

```python
import functools

import jax
import jax.numpy as jnp
from jax import lax
from jax.experimental import pallas as pl
from jax.experimental.pallas import tpu as pltpu
from jax.sharding import PartitionSpec as P

UNROLL = 24
PART = 16
MOST = 12
LISTS = 4
MIB = 1024 * 1024


def pair_list(core_ref, order_ref, pointer_ref, column_ref, after_ref, word_ref, count_ref, *, height):
    del after_ref
    core = core_ref[0]
    rows = pointer_ref.shape[0] - 1
    slots = rows // height // 2
    part = slots // 2

    for index in range(LISTS):
        late, own = index // 2, index % 2
        which = core if own else 1 - core

        def one_row(local, number):
            row = (2 * order_ref[late * part + local // height] + which) * height + local % height
            first, last = pointer_ref[row], pointer_ref[row + 1]

            def one_pair(k, _):
                j = first + 2 * k
                both = (j + 1 < last).astype(jnp.int32)
                word_ref[index, number + k] = (
                    j + local * 512 + column_ref[j] * 16384 + column_ref[j + both] * 524288 + (1 + both) * 16777216
                )
                return 0

            pairs = (last - first + 1) // 2
            lax.fori_loop(0, pairs, one_pair, 0)
            return number + pairs

        total = lax.fori_loop(0, part * height, one_row, 0)
        last = word_ref[index, total - 1] & 16383
        for k in range(UNROLL):
            word_ref[index, total + k] = last
        count_ref[index] = (total + UNROLL - 1) // UNROLL


def make_lists(core, order, pointer, columns, after, height):
    rows = pointer.shape[0] - 1
    smem = pl.BlockSpec(memory_space=pltpu.SMEM)
    width = (rows // LISTS) * (MOST // 2) + UNROLL
    return pl.pallas_call(
        functools.partial(pair_list, height=height),
        in_specs=[smem] * 4 + [pl.BlockSpec(memory_space=pl.ANY)],
        out_specs=[smem] * 2,
        out_shape=[
            jax.ShapeDtypeStruct((LISTS, width), jnp.int32),
            jax.ShapeDtypeStruct((LISTS,), jnp.int32),
        ],
        compiler_params=pltpu.CompilerParams(vmem_limit_bytes=2 * MIB),
        name="pair_list",
    )(core, order, pointer, columns, after)


def add_pairs(word_ref, count_ref, vector_ref, block_ref, out_ref, index, height, ready, arrive):
    out_ref[...] = jnp.zeros_like(out_ref)

    def body(step, ready):
        ready = arrive((word_ref[index, step * UNROLL + UNROLL - 1] >> 9 & 31) // height + 1, ready)
        for k in range(UNROLL):
            word = word_ref[index, step * UNROLL + k]
            j = word & 511
            row = (word >> 9) & 31
            c1 = (word >> 14) & 31
            c2 = (word >> 19) & 31
            n = word >> 24
            left = jnp.concatenate([block_ref[j], block_ref[j + (n >> 1)]], axis=1)
            v1 = vector_ref[c1]
            v2 = vector_ref[c2]
            right = jnp.concatenate([jnp.where(n > 0, v1, jnp.zeros_like(v1)), jnp.where(n > 1, v2, jnp.zeros_like(v2))], axis=0)
            out_ref[row] += jnp.dot(left, right, preferred_element_type=jnp.float32)
        return ready

    return lax.fori_loop(0, count_ref[index], body, ready)


def first_kernel(order_ref, pointer_ref, word_ref, count_ref, vector_ref, source_ref, out_ref, block_ref, sem, *, height):
    capacity = source_ref.shape[0]
    slots = order_ref.shape[0]

    def span(slot):
        row = 2 * order_ref[slot] * height
        first, last = pointer_ref[row], pointer_ref[row + 2 * height]
        return first, (last - first + PART - 1) // PART

    def copy(slot, first, k):
        part = pl.ds(jnp.minimum(first + k * PART, capacity - PART), PART)
        return pltpu.make_async_copy(source_ref.at[part], block_ref.at[part], sem.at[slot, k])

    def start(slot, _):
        first, parts = span(slot)

        def one(k, _):
            copy(slot, first, k).start()
            return 0

        return lax.fori_loop(0, parts, one, 0)

    def wait(slot, _):
        first, parts = span(slot)

        def one(k, _):
            copy(slot, first, k).wait()
            return 0

        return lax.fori_loop(0, parts, one, 0)

    def arrive(needed, ready):
        lax.fori_loop(ready, needed, wait, 0)
        return needed

    lax.fori_loop(0, slots, start, 0)
    ready = add_pairs(word_ref, count_ref, vector_ref, block_ref, out_ref, 0, height, 0, arrive)
    lax.fori_loop(ready, slots, wait, 0)


def some_kernel(word_ref, count_ref, vector_ref, block_ref, out_ref, *, index, height):
    add_pairs(word_ref, count_ref, vector_ref, block_ref, out_ref, index, height, 0, lambda needed, ready: ready)


def first_terms(order, pointer, words, counts, vector, tile_blocks, height):
    smem = pl.BlockSpec(memory_space=pltpu.SMEM)
    vmem = pl.BlockSpec(memory_space=pltpu.VMEM)
    rows = (pointer.shape[0] - 1) // LISTS
    return pl.pallas_call(
        functools.partial(first_kernel, height=height),
        in_specs=[smem] * 4 + [vmem, pl.BlockSpec(memory_space=pl.ANY)],
        out_specs=[vmem, vmem],
        out_shape=[
            jax.ShapeDtypeStruct((rows, tile_blocks.shape[1], vector.shape[2]), jnp.float32),
            pltpu.VMEM(tile_blocks.shape, tile_blocks.dtype),
        ],
        scratch_shapes=[pltpu.SemaphoreType.DMA((order.shape[0], 2 * height * MOST // PART))],
        compiler_params=pltpu.CompilerParams(vmem_limit_bytes=24 * MIB),
        name="first_terms",
    )(order, pointer, words, counts, vector, pltpu.with_memory_space_constraint(tile_blocks, pltpu.HBM))


def some_terms(words, counts, vector, held, index, rows, height):
    smem = pl.BlockSpec(memory_space=pltpu.SMEM)
    vmem = pl.BlockSpec(memory_space=pltpu.VMEM)
    size = held.shape[1]
    return pl.pallas_call(
        functools.partial(some_kernel, index=index, height=height),
        in_specs=[smem, smem, vmem, vmem],
        out_specs=vmem,
        out_shape=jax.ShapeDtypeStruct((rows, size, vector.shape[2]), jnp.float32),
        compiler_params=pltpu.CompilerParams(vmem_limit_bytes=24 * MIB),
        cost_estimate=pl.CostEstimate(
            flops=2 * rows * 8 * size**3, bytes_accessed=rows * 8 * size * size, transcendentals=0
        ),
        name="some_terms",
    )(words, counts, vector, pltpu.with_memory_space_constraint(held, pltpu.VMEM))


def combine_kernel(*refs):
    *terms, out_ref = refs
    chips, taller, width = out_ref.shape
    rows, size, _ = terms[0].shape
    height = rows // chips
    step = 32
    tops = []
    for chip in range(chips):
        most = jnp.zeros((step, width), jnp.float32)
        for k in range(height):
            row = chip * height + k
            for t in range(0, size, step):
                both = terms[0][row, t : t + step]
                for term in terms[1:]:
                    both = both + term[row, t : t + step]
                out_ref[chip, k * size + t : k * size + t + step] = both
                most = jnp.maximum(most, jnp.abs(both))
        tops.append(jnp.max(most, axis=0, keepdims=True))
    most = jnp.max(jnp.concatenate(tops, axis=0), axis=1, keepdims=True)
    power = jnp.floor(jnp.log2(jnp.maximum(most, 1e-30))) - 14.0
    power = jnp.broadcast_to(power, (chips, width))
    scale = jnp.exp2(-power)
    for chip in range(chips):
        by = jnp.broadcast_to(scale[chip : chip + 1], (step, width))
        for t in range(0, height * size, step):
            out_ref[chip, t : t + step] = out_ref[chip, t : t + step] * by
        out_ref[chip, height * size :] = jnp.broadcast_to(power[chip : chip + 1], (taller - height * size, width))


def combine(chips, *terms):
    vmem = pl.BlockSpec(memory_space=pltpu.VMEM)
    rows, size, width = terms[0].shape
    return pl.pallas_call(
        combine_kernel,
        in_specs=[vmem] * len(terms),
        out_specs=vmem,
        out_shape=jax.ShapeDtypeStruct((chips, rows // chips * size + 8, width), jnp.float32),
        compiler_params=pltpu.CompilerParams(vmem_limit_bytes=24 * MIB),
        name="combine",
    )(*terms)


def per_device(subspace, blocks, row_pointer, block_column):
    tile_blocks = blocks[0, 0]
    pointer = row_pointer[0, 0]
    size = tile_blocks.shape[1]
    own_rows, width = subspace.shape
    height = own_rows // size
    chips = lax.axis_size("col") // 2
    core = lax.axis_index("col") % 2
    swap = [(c, c ^ 1) for c in range(2 * chips)]
    ring = lax.axis_size("row") // 2
    here = lax.axis_index("row")
    loop = chips // 2
    chip = lax.axis_index("col") // 2

    source = block_column[0, 0] // height
    apart = (source - here) % ring
    same = jnp.where(apart == 0, 0, jnp.where(apart == 1, 3, jnp.where(apart == 2, 6, 2)))
    other = jnp.where(apart == 0, 1, jnp.where(apart == 1, 5, jnp.where(apart == 2, 7, 4)))
    slot = jnp.where(source // ring == here // ring, same, other)
    place = (slot * height + block_column[0, 0] % height).astype(jnp.int32)

    k = jnp.arange(chips, dtype=jnp.int32)
    away_z = ((k == 0) | (k == 1) | (k == 3) | (k == 5)).astype(jnp.int32)
    away_y = jnp.where((k == 0) | (k == 6), 1, jnp.where((k == 1) | (k == 7), 3, jnp.where((k == 2) | (k == 3), 2, 0)))
    order = (chip // loop + away_z) % 2 * loop + (chip + away_y) % loop
    order = order.astype(jnp.int32)

    def shift(x, dz, dx):
        pairs = [(z * ring + k, (z + dz) % 2 * ring + (k + dx) % ring) for z in range(2) for k in range(ring)]
        return lax.ppermute(x, "row", pairs)

    def pass_on(x, dz, dy):
        pairs = []
        for z in range(2):
            for y in range(loop):
                for c in range(2):
                    to = (z + dz) % 2 * loop + (y + dy) % loop
                    pairs.append(((z * loop + y) * 2 + c, to * 2 + c))
        return lax.ppermute(x, "col", pairs)

    def gather(vector):
        below, above, across = shift(vector, 0, 1), shift(vector, 0, -1), shift(vector, 1, 0)
        near = jnp.concatenate([vector, across])
        sides = jnp.concatenate([below, above])
        opposite = shift(near, 0, 2)
        far = shift(sides, 1, 0)
        return jnp.concatenate([near, sides, far, opposite]).reshape(-1, size, width), sides

    def widened(x):
        weight = jnp.exp2(x[:, own_rows : own_rows + 1].astype(jnp.float32))
        return x[:, :own_rows].astype(jnp.float32) * weight

    def multiply(vector, lists, held):
        gathered, sides = gather(vector)
        if lists is None:
            lists = make_lists(core.reshape(1), order, pointer, place, sides, height)
        words, counts = lists
        rows = loop * height
        if held is None:
            given, held = first_terms(order, pointer, words, counts, gathered, tile_blocks, height)
        else:
            given = some_terms(words, counts, gathered, held, 0, rows, height)
        taken = lax.ppermute(given, "col", swap)
        kept = some_terms(words, counts, gathered, held, 1, rows, height)
        early = combine(loop, kept, taken).astype(jnp.float16)
        across = pass_on(early[:2], 1, 0)
        opposite = pass_on(early[2:], 0, 2)
        given = some_terms(words, counts, gathered, held, 2, rows, height)
        taken = lax.ppermute(given, "col", swap)
        kept = some_terms(words, counts, gathered, held, 3, rows, height)
        passed = jnp.concatenate([widened(opposite), widened(across)]).reshape(kept.shape)
        late = combine(loop, kept, taken, passed)
        half = late.astype(jnp.float16)
        parts = [pass_on(half[1:2], 1, 0), pass_on(half[2:3], 0, 1), pass_on(half[3:4], 0, -1)]
        total = widened(late[:1])
        for part in parts:
            total = total + widened(part)
        return total[0], lists, held

    total, lists, held = multiply(subspace, None, None)
    first = total.astype(jnp.bfloat16)
    total, lists, held = multiply(first, lists, held)
    second = (2.0 * total - subspace.astype(jnp.float32)).astype(jnp.bfloat16)
    total, lists, held = multiply(second, lists, held)
    return 2.0 * total - first.astype(jnp.float32)


def solution(mesh):
    placed = (
        P(("row", "col"), None),
        P("row", "col", None, None, None),
        P("row", "col", None),
        P("row", "col", None),
    )
    return jax.shard_map(
        per_device, mesh=mesh, in_specs=placed, out_specs=P(("row", "col"), None), check_vma=False
    )
```

```python
import functools

import jax
import jax.numpy as jnp
from jax import lax
from jax.experimental import pallas as pl
from jax.experimental.pallas import tpu as pltpu
from jax.sharding import PartitionSpec as P

UNROLL = 24
PART = 16
MOST = 12
LISTS = 4
MIB = 1024 * 1024


def pair_list(core_ref, order_ref, pointer_ref, column_ref, after_ref, word_ref, count_ref, *, height):
    del after_ref
    core = core_ref[0]
    rows = pointer_ref.shape[0] - 1
    slots = rows // height // 2
    part = slots // 2

    for index in range(LISTS):
        late, own = index // 2, index % 2
        which = core if own else 1 - core

        def one_row(local, number):
            row = (2 * order_ref[late * part + local // height] + which) * height + local % height
            first, last = pointer_ref[row], pointer_ref[row + 1]

            def one_pair(k, _):
                j = first + 2 * k
                both = (j + 1 < last).astype(jnp.int32)
                word_ref[index, number + k] = (
                    j + local * 512 + column_ref[j] * 16384 + column_ref[j + both] * 524288 + (1 + both) * 16777216
                )
                return 0

            pairs = (last - first + 1) // 2
            lax.fori_loop(0, pairs, one_pair, 0)
            return number + pairs

        total = lax.fori_loop(0, part * height, one_row, 0)
        last = word_ref[index, total - 1] & 16383
        for k in range(UNROLL):
            word_ref[index, total + k] = last
        count_ref[index] = (total + UNROLL - 1) // UNROLL


def make_lists(core, order, pointer, columns, after, height):
    rows = pointer.shape[0] - 1
    smem = pl.BlockSpec(memory_space=pltpu.SMEM)
    width = (rows // LISTS) * (MOST // 2) + UNROLL
    return pl.pallas_call(
        functools.partial(pair_list, height=height),
        in_specs=[smem] * 4 + [pl.BlockSpec(memory_space=pl.ANY)],
        out_specs=[smem] * 2,
        out_shape=[
            jax.ShapeDtypeStruct((LISTS, width), jnp.int32),
            jax.ShapeDtypeStruct((LISTS,), jnp.int32),
        ],
        compiler_params=pltpu.CompilerParams(vmem_limit_bytes=2 * MIB),
        name="pair_list",
    )(core, order, pointer, columns, after)


def add_pairs(word_ref, count_ref, vector_ref, block_ref, out_ref, index, height, ready, arrive):
    out_ref[...] = jnp.zeros_like(out_ref)

    def body(step, ready):
        ready = arrive((word_ref[index, step * UNROLL + UNROLL - 1] >> 9 & 31) // height + 1, ready)
        for k in range(UNROLL):
            word = word_ref[index, step * UNROLL + k]
            j = word & 511
            row = (word >> 9) & 31
            c1 = (word >> 14) & 31
            c2 = (word >> 19) & 31
            n = word >> 24
            left = jnp.concatenate([block_ref[j], block_ref[j + (n >> 1)]], axis=1)
            v1 = vector_ref[c1]
            v2 = vector_ref[c2]
            right = jnp.concatenate([jnp.where(n > 0, v1, jnp.zeros_like(v1)), jnp.where(n > 1, v2, jnp.zeros_like(v2))], axis=0)
            out_ref[row] += jnp.dot(left, right, preferred_element_type=jnp.float32)
        return ready

    return lax.fori_loop(0, count_ref[index], body, ready)


def first_kernel(order_ref, pointer_ref, word_ref, count_ref, vector_ref, source_ref, out_ref, block_ref, sem, *, height):
    capacity = source_ref.shape[0]
    slots = order_ref.shape[0]

    def span(slot):
        row = 2 * order_ref[slot] * height
        first, last = pointer_ref[row], pointer_ref[row + 2 * height]
        return first, (last - first + PART - 1) // PART

    def copy(slot, first, k):
        part = pl.ds(jnp.minimum(first + k * PART, capacity - PART), PART)
        return pltpu.make_async_copy(source_ref.at[part], block_ref.at[part], sem.at[slot, k])

    def start(slot, _):
        first, parts = span(slot)

        def one(k, _):
            copy(slot, first, k).start()
            return 0

        return lax.fori_loop(0, parts, one, 0)

    def wait(slot, _):
        first, parts = span(slot)

        def one(k, _):
            copy(slot, first, k).wait()
            return 0

        return lax.fori_loop(0, parts, one, 0)

    def arrive(needed, ready):
        lax.fori_loop(ready, needed, wait, 0)
        return needed

    lax.fori_loop(0, slots, start, 0)
    ready = add_pairs(word_ref, count_ref, vector_ref, block_ref, out_ref, 0, height, 0, arrive)
    lax.fori_loop(ready, slots, wait, 0)


def some_kernel(word_ref, count_ref, vector_ref, block_ref, out_ref, *, index, height):
    add_pairs(word_ref, count_ref, vector_ref, block_ref, out_ref, index, height, 0, lambda needed, ready: ready)


def first_terms(order, pointer, words, counts, vector, tile_blocks, height):
    smem = pl.BlockSpec(memory_space=pltpu.SMEM)
    vmem = pl.BlockSpec(memory_space=pltpu.VMEM)
    rows = (pointer.shape[0] - 1) // LISTS
    return pl.pallas_call(
        functools.partial(first_kernel, height=height),
        in_specs=[smem] * 4 + [vmem, pl.BlockSpec(memory_space=pl.ANY)],
        out_specs=[vmem, vmem],
        out_shape=[
            jax.ShapeDtypeStruct((rows, tile_blocks.shape[1], vector.shape[2]), jnp.float32),
            pltpu.VMEM(tile_blocks.shape, tile_blocks.dtype),
        ],
        scratch_shapes=[pltpu.SemaphoreType.DMA((order.shape[0], 2 * height * MOST // PART))],
        compiler_params=pltpu.CompilerParams(vmem_limit_bytes=24 * MIB),
        name="first_terms",
    )(order, pointer, words, counts, vector, pltpu.with_memory_space_constraint(tile_blocks, pltpu.HBM))


def some_terms(words, counts, vector, held, index, rows, height):
    smem = pl.BlockSpec(memory_space=pltpu.SMEM)
    vmem = pl.BlockSpec(memory_space=pltpu.VMEM)
    size = held.shape[1]
    return pl.pallas_call(
        functools.partial(some_kernel, index=index, height=height),
        in_specs=[smem, smem, vmem, vmem],
        out_specs=vmem,
        out_shape=jax.ShapeDtypeStruct((rows, size, vector.shape[2]), jnp.float32),
        compiler_params=pltpu.CompilerParams(vmem_limit_bytes=24 * MIB),
        cost_estimate=pl.CostEstimate(
            flops=2 * rows * 64 * size**3, bytes_accessed=rows * 8 * size * size, transcendentals=0
        ),
        name="some_terms",
    )(words, counts, vector, pltpu.with_memory_space_constraint(held, pltpu.VMEM))


def combine_kernel(*refs):
    *terms, out_ref = refs
    chips, taller, width = out_ref.shape
    rows, size, _ = terms[0].shape
    height = rows // chips
    step = 32
    tops = []
    for chip in range(chips):
        most = jnp.zeros((step, width), jnp.float32)
        for k in range(height):
            row = chip * height + k
            for t in range(0, size, step):
                both = terms[0][row, t : t + step]
                for term in terms[1:]:
                    both = both + term[row, t : t + step]
                out_ref[chip, k * size + t : k * size + t + step] = both
                most = jnp.maximum(most, jnp.abs(both))
        tops.append(jnp.max(most, axis=0, keepdims=True))
    most = jnp.max(jnp.concatenate(tops, axis=0), axis=1, keepdims=True)
    power = jnp.floor(jnp.log2(jnp.maximum(most, 1e-30))) - 14.0
    power = jnp.broadcast_to(power, (chips, width))
    scale = jnp.exp2(-power)
    for chip in range(chips):
        by = jnp.broadcast_to(scale[chip : chip + 1], (step, width))
        for t in range(0, height * size, step):
            out_ref[chip, t : t + step] = out_ref[chip, t : t + step] * by
        out_ref[chip, height * size :] = jnp.broadcast_to(power[chip : chip + 1], (taller - height * size, width))


def combine(chips, *terms):
    vmem = pl.BlockSpec(memory_space=pltpu.VMEM)
    rows, size, width = terms[0].shape
    return pl.pallas_call(
        combine_kernel,
        in_specs=[vmem] * len(terms),
        out_specs=vmem,
        out_shape=jax.ShapeDtypeStruct((chips, rows // chips * size + 8, width), jnp.float32),
        compiler_params=pltpu.CompilerParams(vmem_limit_bytes=24 * MIB),
        name="combine",
    )(*terms)


def per_device(subspace, blocks, row_pointer, block_column):
    tile_blocks = blocks[0, 0]
    pointer = row_pointer[0, 0]
    size = tile_blocks.shape[1]
    own_rows, width = subspace.shape
    height = own_rows // size
    chips = lax.axis_size("col") // 2
    core = lax.axis_index("col") % 2
    swap = [(c, c ^ 1) for c in range(2 * chips)]
    ring = lax.axis_size("row") // 2
    here = lax.axis_index("row")
    loop = chips // 2
    chip = lax.axis_index("col") // 2

    source = block_column[0, 0] // height
    apart = (source - here) % ring
    same = jnp.where(apart == 0, 0, jnp.where(apart == 1, 3, jnp.where(apart == 2, 6, 2)))
    other = jnp.where(apart == 0, 1, jnp.where(apart == 1, 5, jnp.where(apart == 2, 7, 4)))
    slot = jnp.where(source // ring == here // ring, same, other)
    place = (slot * height + block_column[0, 0] % height).astype(jnp.int32)

    k = jnp.arange(chips, dtype=jnp.int32)
    away_z = ((k == 0) | (k == 1) | (k == 3) | (k == 5)).astype(jnp.int32)
    away_y = jnp.where((k == 0) | (k == 6), 1, jnp.where((k == 1) | (k == 7), 3, jnp.where((k == 2) | (k == 3), 2, 0)))
    order = (chip // loop + away_z) % 2 * loop + (chip + away_y) % loop
    order = order.astype(jnp.int32)

    def shift(x, dz, dx):
        pairs = [(z * ring + k, (z + dz) % 2 * ring + (k + dx) % ring) for z in range(2) for k in range(ring)]
        return lax.ppermute(x, "row", pairs)

    def pass_on(x, dz, dy):
        pairs = []
        for z in range(2):
            for y in range(loop):
                for c in range(2):
                    to = (z + dz) % 2 * loop + (y + dy) % loop
                    pairs.append(((z * loop + y) * 2 + c, to * 2 + c))
        return lax.ppermute(x, "col", pairs)

    def gather(vector):
        below, above, across = shift(vector, 0, 1), shift(vector, 0, -1), shift(vector, 1, 0)
        near = jnp.concatenate([vector, across])
        sides = jnp.concatenate([below, above])
        opposite = shift(near, 0, 2)
        far = shift(sides, 1, 0)
        return jnp.concatenate([near, sides, far, opposite]).reshape(-1, size, width), sides

    def widened(x):
        weight = jnp.exp2(x[:, own_rows : own_rows + 1].astype(jnp.float32))
        return x[:, :own_rows].astype(jnp.float32) * weight

    def multiply(vector, lists, held):
        gathered, sides = gather(vector)
        if lists is None:
            lists = make_lists(core.reshape(1), order, pointer, place, sides, height)
        words, counts = lists
        rows = loop * height
        if held is None:
            given, held = first_terms(order, pointer, words, counts, gathered, tile_blocks, height)
        else:
            given = some_terms(words, counts, gathered, held, 0, rows, height)
        taken = lax.ppermute(given, "col", swap)
        kept = some_terms(words, counts, gathered, held, 1, rows, height)
        early = combine(loop, kept, taken).astype(jnp.float16)
        across = pass_on(early[:2], 1, 0)
        opposite = pass_on(early[2:], 0, 2)
        given = some_terms(words, counts, gathered, held, 2, rows, height)
        taken = lax.ppermute(given, "col", swap)
        kept = some_terms(words, counts, gathered, held, 3, rows, height)
        passed = jnp.concatenate([widened(opposite), widened(across)]).reshape(kept.shape)
        late = combine(loop, kept, taken, passed)
        half = late.astype(jnp.float16)
        parts = [pass_on(half[1:2], 1, 0), pass_on(half[2:3], 0, 1), pass_on(half[3:4], 0, -1)]
        total = widened(late[:1])
        for part in parts:
            total = total + widened(part)
        return total[0], lists, held

    total, lists, held = multiply(subspace, None, None)
    first = total.astype(jnp.bfloat16)
    total, lists, held = multiply(first, lists, held)
    second = (2.0 * total - subspace.astype(jnp.float32)).astype(jnp.bfloat16)
    total, lists, held = multiply(second, lists, held)
    return 2.0 * total - first.astype(jnp.float32)


def solution(mesh):
    placed = (
        P(("row", "col"), None),
        P("row", "col", None, None, None),
        P("row", "col", None),
        P("row", "col", None),
    )
    return jax.shard_map(
        per_device, mesh=mesh, in_specs=placed, out_specs=P(("row", "col"), None), check_vma=False
    )
```

```python
import functools

import jax
import jax.numpy as jnp
from jax import lax
from jax.experimental import pallas as pl
from jax.experimental.pallas import tpu as pltpu
from jax.sharding import PartitionSpec as P

UNROLL = 24
PART = 16
MOST = 12
LISTS = 4
MIB = 1024 * 1024


def pair_list(core_ref, order_ref, pointer_ref, column_ref, after_ref, word_ref, count_ref, *, height):
    del after_ref
    core = core_ref[0]
    rows = pointer_ref.shape[0] - 1
    slots = rows // height // 2
    part = slots // 2

    for index in range(LISTS):
        late, own = index // 2, index % 2
        which = core if own else 1 - core

        def one_row(local, number):
            row = (2 * order_ref[late * part + local // height] + which) * height + local % height
            first, last = pointer_ref[row], pointer_ref[row + 1]

            def one_pair(k, _):
                j = first + 2 * k
                both = (j + 1 < last).astype(jnp.int32)
                word_ref[index, number + k] = (
                    j + local * 512 + column_ref[j] * 16384 + column_ref[j + both] * 524288 + (1 + both) * 16777216
                    + (k == 0).astype(jnp.int32) * 67108864
                )
                return 0

            pairs = (last - first + 1) // 2
            lax.fori_loop(0, pairs, one_pair, 0)
            return number + pairs

        total = lax.fori_loop(0, part * height, one_row, 0)
        last = word_ref[index, total - 1] & 16383
        for k in range(UNROLL):
            word_ref[index, total + k] = last
        count_ref[index] = (total + UNROLL - 1) // UNROLL


def make_lists(core, order, pointer, columns, after, height):
    rows = pointer.shape[0] - 1
    smem = pl.BlockSpec(memory_space=pltpu.SMEM)
    width = (rows // LISTS) * (MOST // 2) + UNROLL
    return pl.pallas_call(
        functools.partial(pair_list, height=height),
        in_specs=[smem] * 4 + [pl.BlockSpec(memory_space=pl.ANY)],
        out_specs=[smem] * 2,
        out_shape=[
            jax.ShapeDtypeStruct((LISTS, width), jnp.int32),
            jax.ShapeDtypeStruct((LISTS,), jnp.int32),
        ],
        compiler_params=pltpu.CompilerParams(vmem_limit_bytes=2 * MIB),
        name="pair_list",
    )(core, order, pointer, columns, after)


def add_pairs(word_ref, count_ref, vector_ref, block_ref, out_ref, index, height, ready, arrive):
    def body(step, state):
        ready, total = state
        ready = arrive((word_ref[index, step * UNROLL + UNROLL - 1] >> 9 & 31) // height + 1, ready)
        for k in range(UNROLL):
            word = word_ref[index, step * UNROLL + k]
            j = word & 511
            row = (word >> 9) & 31
            c1 = (word >> 14) & 31
            c2 = (word >> 19) & 31
            n = (word >> 24) & 3
            left = jnp.concatenate([block_ref[j], block_ref[j + (n >> 1)]], axis=1)
            v1 = vector_ref[c1]
            v2 = vector_ref[c2]
            right = jnp.concatenate([jnp.where(n > 0, v1, jnp.zeros_like(v1)), jnp.where(n > 1, v2, jnp.zeros_like(v2))], axis=0)
            total = jnp.where(word >> 26 > 0, jnp.zeros_like(total), total)
            total += jnp.dot(left, right, preferred_element_type=jnp.float32)
            out_ref[row] = total
        return ready, total

    empty = jnp.zeros(out_ref.shape[1:], out_ref.dtype)
    return lax.fori_loop(0, count_ref[index], body, (ready, empty))[0]


def first_kernel(order_ref, pointer_ref, word_ref, count_ref, vector_ref, source_ref, out_ref, block_ref, sem, *, height):
    capacity = source_ref.shape[0]
    slots = order_ref.shape[0]

    def span(slot):
        row = 2 * order_ref[slot] * height
        first, last = pointer_ref[row], pointer_ref[row + 2 * height]
        return first, (last - first + PART - 1) // PART

    def copy(slot, first, k):
        part = pl.ds(jnp.minimum(first + k * PART, capacity - PART), PART)
        return pltpu.make_async_copy(source_ref.at[part], block_ref.at[part], sem.at[slot, k])

    def start(slot, _):
        first, parts = span(slot)

        def one(k, _):
            copy(slot, first, k).start()
            return 0

        return lax.fori_loop(0, parts, one, 0)

    def wait(slot, _):
        first, parts = span(slot)

        def one(k, _):
            copy(slot, first, k).wait()
            return 0

        return lax.fori_loop(0, parts, one, 0)

    def arrive(needed, ready):
        lax.fori_loop(ready, needed, wait, 0)
        return needed

    lax.fori_loop(0, slots, start, 0)
    ready = add_pairs(word_ref, count_ref, vector_ref, block_ref, out_ref, 0, height, 0, arrive)
    lax.fori_loop(ready, slots, wait, 0)


def some_kernel(word_ref, count_ref, vector_ref, block_ref, out_ref, *, index, height):
    add_pairs(word_ref, count_ref, vector_ref, block_ref, out_ref, index, height, 0, lambda needed, ready: ready)


def first_terms(order, pointer, words, counts, vector, tile_blocks, height):
    smem = pl.BlockSpec(memory_space=pltpu.SMEM)
    vmem = pl.BlockSpec(memory_space=pltpu.VMEM)
    rows = (pointer.shape[0] - 1) // LISTS
    return pl.pallas_call(
        functools.partial(first_kernel, height=height),
        in_specs=[smem] * 4 + [vmem, pl.BlockSpec(memory_space=pl.ANY)],
        out_specs=[vmem, vmem],
        out_shape=[
            jax.ShapeDtypeStruct((rows, tile_blocks.shape[1], vector.shape[2]), jnp.float32),
            pltpu.VMEM(tile_blocks.shape, tile_blocks.dtype),
        ],
        scratch_shapes=[pltpu.SemaphoreType.DMA((order.shape[0], 2 * height * MOST // PART))],
        compiler_params=pltpu.CompilerParams(vmem_limit_bytes=24 * MIB),
        name="first_terms",
    )(order, pointer, words, counts, vector, pltpu.with_memory_space_constraint(tile_blocks, pltpu.HBM))


def hold_kernel(from_ref, to_ref):
    to_ref[...] = from_ref[...]


def hold(x):
    vmem = pl.BlockSpec(memory_space=pltpu.VMEM)
    return pl.pallas_call(
        hold_kernel,
        in_specs=[vmem],
        out_specs=vmem,
        out_shape=pltpu.VMEM(x.shape, x.dtype),
        compiler_params=pltpu.CompilerParams(vmem_limit_bytes=2 * MIB),
        name="hold",
    )(x)


def some_terms(words, counts, vector, held, index, rows, height):
    smem = pl.BlockSpec(memory_space=pltpu.SMEM)
    vmem = pl.BlockSpec(memory_space=pltpu.VMEM)
    size = held.shape[1]
    return pl.pallas_call(
        functools.partial(some_kernel, index=index, height=height),
        in_specs=[smem, smem, vmem, vmem],
        out_specs=vmem,
        out_shape=jax.ShapeDtypeStruct((rows, size, vector.shape[2]), jnp.float32),
        compiler_params=pltpu.CompilerParams(vmem_limit_bytes=24 * MIB),
        cost_estimate=pl.CostEstimate(
            flops=2 * rows * 64 * size**3, bytes_accessed=rows * 8 * size * size, transcendentals=0
        ),
        name="some_terms",
    )(words, counts, vector, pltpu.with_memory_space_constraint(held, pltpu.VMEM))


def combine_kernel(*refs):
    *terms, out_ref = refs
    chips, taller, width = out_ref.shape
    rows, size, _ = terms[0].shape
    height = rows // chips
    step = 32
    tops = []
    for chip in range(chips):
        most = jnp.zeros((step, width), jnp.float32)
        for k in range(height):
            row = chip * height + k
            for t in range(0, size, step):
                both = terms[0][row, t : t + step]
                for term in terms[1:]:
                    both = both + term[row, t : t + step]
                out_ref[chip, k * size + t : k * size + t + step] = both
                most = jnp.maximum(most, jnp.abs(both))
        tops.append(jnp.max(most, axis=0, keepdims=True))
    most = jnp.max(jnp.concatenate(tops, axis=0), axis=1, keepdims=True)
    power = jnp.floor(jnp.log2(jnp.maximum(most, 1e-30))) - 14.0
    power = jnp.broadcast_to(power, (chips, width))
    scale = jnp.exp2(-power)
    for chip in range(chips):
        by = jnp.broadcast_to(scale[chip : chip + 1], (step, width))
        for t in range(0, height * size, step):
            out_ref[chip, t : t + step] = out_ref[chip, t : t + step] * by
        out_ref[chip, height * size :] = jnp.broadcast_to(power[chip : chip + 1], (taller - height * size, width))


def combine(chips, *terms):
    vmem = pl.BlockSpec(memory_space=pltpu.VMEM)
    rows, size, width = terms[0].shape
    return pl.pallas_call(
        combine_kernel,
        in_specs=[vmem] * len(terms),
        out_specs=vmem,
        out_shape=jax.ShapeDtypeStruct((chips, rows // chips * size + 8, width), jnp.float32),
        compiler_params=pltpu.CompilerParams(vmem_limit_bytes=24 * MIB),
        name="combine",
    )(*terms)


def per_device(subspace, blocks, row_pointer, block_column):
    tile_blocks = blocks[0, 0]
    pointer = row_pointer[0, 0]
    size = tile_blocks.shape[1]
    own_rows, width = subspace.shape
    height = own_rows // size
    chips = lax.axis_size("col") // 2
    core = lax.axis_index("col") % 2
    swap = [(c, c ^ 1) for c in range(2 * chips)]
    ring = lax.axis_size("row") // 2
    here = lax.axis_index("row")
    loop = chips // 2
    chip = lax.axis_index("col") // 2

    source = block_column[0, 0] // height
    apart = (source - here) % ring
    same = jnp.where(apart == 0, 0, jnp.where(apart == 1, 3, jnp.where(apart == 2, 6, 2)))
    other = jnp.where(apart == 0, 1, jnp.where(apart == 1, 5, jnp.where(apart == 2, 7, 4)))
    slot = jnp.where(source // ring == here // ring, same, other)
    place = (slot * height + block_column[0, 0] % height).astype(jnp.int32)

    k = jnp.arange(chips, dtype=jnp.int32)
    away_z = ((k == 0) | (k == 1) | (k == 3) | (k == 5)).astype(jnp.int32)
    away_y = jnp.where((k == 0) | (k == 6), 1, jnp.where((k == 1) | (k == 7), 3, jnp.where((k == 2) | (k == 3), 2, 0)))
    order = (chip // loop + away_z) % 2 * loop + (chip + away_y) % loop
    order = order.astype(jnp.int32)

    def shift(x, dz, dx):
        pairs = [(z * ring + k, (z + dz) % 2 * ring + (k + dx) % ring) for z in range(2) for k in range(ring)]
        return lax.ppermute(x, "row", pairs)

    def pass_on(x, dz, dy):
        pairs = []
        for z in range(2):
            for y in range(loop):
                for c in range(2):
                    to = (z + dz) % 2 * loop + (y + dy) % loop
                    pairs.append(((z * loop + y) * 2 + c, to * 2 + c))
        return lax.ppermute(x, "col", pairs)

    def gather(vector, near_vector):
        below, above, across = shift(vector, 0, 1), shift(vector, 0, -1), shift(vector, 1, 0)
        near = jnp.concatenate([near_vector, across])
        sides = jnp.concatenate([below, above])
        opposite = shift(near, 0, 2)
        far = shift(sides, 1, 0)
        return jnp.concatenate([near, sides, far, opposite]).reshape(-1, size, width), sides

    def widened(x):
        weight = jnp.exp2(x[:, own_rows : own_rows + 1].astype(jnp.float32))
        return x[:, :own_rows].astype(jnp.float32) * weight

    def multiply(vector, lists, held):
        gathered, sides = gather(vector, hold(vector) if lists is None else vector)
        if lists is None:
            lists = make_lists(core.reshape(1), order, pointer, place, sides, height)
        words, counts = lists
        rows = loop * height
        if held is None:
            given, held = first_terms(order, pointer, words, counts, gathered, tile_blocks, height)
        else:
            given = some_terms(words, counts, gathered, held, 0, rows, height)
        taken = lax.ppermute(given, "col", swap)
        kept = some_terms(words, counts, gathered, held, 1, rows, height)
        early = combine(loop, kept, taken).astype(jnp.float16)
        across = pass_on(early[:2], 1, 0)
        opposite = pass_on(early[2:], 0, 2)
        given = some_terms(words, counts, gathered, held, 2, rows, height)
        taken = lax.ppermute(given, "col", swap)
        kept = some_terms(words, counts, gathered, held, 3, rows, height)
        passed = jnp.concatenate([widened(opposite), widened(across)]).reshape(kept.shape)
        late = combine(loop, kept, taken, passed)
        half = late.astype(jnp.float16)
        parts = [pass_on(half[1:2], 1, 0), pass_on(half[2:3], 0, 1), pass_on(half[3:4], 0, -1)]
        total = widened(late[:1])
        for part in parts:
            total = total + widened(part)
        return total[0], lists, held

    total, lists, held = multiply(subspace, None, None)
    first = total.astype(jnp.bfloat16)
    total, lists, held = multiply(first, lists, held)
    second = (2.0 * total - subspace.astype(jnp.float32)).astype(jnp.bfloat16)
    total, lists, held = multiply(second, lists, held)
    return 2.0 * total - first.astype(jnp.float32)


def solution(mesh):
    placed = (
        P(("row", "col"), None),
        P("row", "col", None, None, None),
        P("row", "col", None),
        P("row", "col", None),
    )
    return jax.shard_map(
        per_device, mesh=mesh, in_specs=placed, out_specs=P(("row", "col"), None), check_vma=False
    )
```
